32 devices in a mesh: query: 8 (over z, x), head: 4 (over y, core).
Axes of the slice: x: 2, y: 2, z: 4, core: 2. Of those that a mesh axis runs over, the one named last changes fastest.
Arguments:
- queries: bfloat16 [8192, 4096], P('query', 'head'), may hold values from -12 to 12
- mem_keys: bfloat16 [512, 4096], P('head'), may hold values from -6 to 6
- mem_values: bfloat16 [512, 4096], P('head'), may hold values from -6 to 6
- grad_out: bfloat16 [8192, 4096], P('query', 'head'), may hold values from -3 to 3
Outputs:
- attended: bfloat16 [8192, 4096], P('query', 'head')
- query_gradients: bfloat16 [8192, 4096], P('query', 'head')
- grad_keys: bfloat16 [512, 4096], P(('query', 'head'))
- grad_values: bfloat16 [512, 4096], P(('query', 'head'))
The draws below stay inside these ranges and needn't reach their ends.
All inputs are finite; a program needn't handle non-finite values.
Results may differ from the reference program's by a relative error of at most 0.025.
Values may be sent and summed in bfloat16 or wider, within the bound.
A program may use at most 64 MiB of HBM per device.

```python
import jax
import jax.numpy as jnp
from jax import lax

HEADS = 16
HEAD_DIM = 256
WIDTH = 4096
ROWS = 8192
MEMORY = 512


def draw_queries(key, part):
    key = jax.random.fold_in(key, 5)
    first_key = jax.random.fold_in(key, 0)
    values = jax.random.normal(first_key, (ROWS, WIDTH), jnp.float32) * 2.5
    return jnp.clip(values, -12.0, 12.0).astype(jnp.bfloat16)


def draw_mem_keys(key, part):
    key = jax.random.fold_in(key, 11)
    first_key = jax.random.fold_in(key, 0)
    values = jax.random.normal(first_key, (MEMORY, WIDTH), jnp.float32)
    return jnp.clip(values, -6.0, 6.0).astype(jnp.bfloat16)


def steps_of(rng, extent, shards, low, largest):
    gain, own = 1.0, jax.random.fold_in(rng, 6)
    for axis_at, parts in shards:
        steps = jnp.exp(jax.random.uniform(jax.random.fold_in(own, axis_at), (parts,), jnp.float32, low / len(shards), largest / len(shards)))
        gain = gain * jnp.repeat(steps, extent[axis_at] // parts).reshape([-1 if axis == axis_at else 1 for axis in range(len(extent))])
    return gain


def scatter_about(key, extent, scale, most, shards=(), dtype=jnp.bfloat16):
    values = jax.random.normal(key, extent, jnp.float32) * scale
    if len(shards) > 0:
        values = steps_of(key, extent, shards, -0.22, 0.18) * values
    return jnp.clip(values, min=-most, max=most).astype(dtype)


def setup_inputs(seed: int = 0) -> dict:
    arg_keys = jax.random.split(jax.random.key(seed), 5)
    queries = draw_queries(jax.random.fold_in(arg_keys[4], 71), 0)
    mem_keys = draw_mem_keys(jax.random.fold_in(arg_keys[4], 71), 0)
    mem_values = scatter_about(arg_keys[2], (MEMORY, WIDTH), 1.0, 6.0, ((0, 4),))
    grad_out = scatter_about(arg_keys[3], (ROWS, WIDTH), 0.5, 3.0, ((0, 8), (1, 4)))
    return {"queries": queries, "mem_keys": mem_keys, "mem_values": mem_values, "grad_out": grad_out}


def one_head(pieces):
    query_h, key_h, value_h, cotan_h = pieces
    score_scale = HEAD_DIM ** -0.5
    scores = jnp.dot(query_h, key_h.T, preferred_element_type=jnp.float32) * score_scale
    row_top = jnp.max(scores, axis=-1, keepdims=True)
    weights = jnp.exp(scores - row_top)
    attention_probabilities = (weights / jnp.sum(weights, axis=-1, keepdims=True)).astype(jnp.bfloat16)
    attended = jnp.dot(attention_probabilities, value_h, preferred_element_type=jnp.float32).astype(jnp.bfloat16)
    dprobs = jnp.dot(cotan_h, value_h.T, preferred_element_type=jnp.float32)
    row_delta = jnp.sum(attention_probabilities.astype(jnp.float32) * dprobs, axis=-1, keepdims=True)
    score_gradients = (attention_probabilities.astype(jnp.float32) * (dprobs - row_delta) * score_scale).astype(jnp.bfloat16)
    grad_query = jnp.dot(score_gradients, key_h, preferred_element_type=jnp.float32).astype(jnp.bfloat16)
    grad_key = jnp.dot(score_gradients.T, query_h, preferred_element_type=jnp.float32).astype(jnp.bfloat16)
    grad_value = jnp.dot(attention_probabilities.T, cotan_h, preferred_element_type=jnp.float32).astype(jnp.bfloat16)
    return attended, grad_query, grad_key, grad_value


def split_heads(array):
    return array.reshape(array.shape[0], HEADS, HEAD_DIM).transpose(1, 0, 2)


def join_heads(array):
    return array.transpose(1, 0, 2).reshape(array.shape[1], HEADS * HEAD_DIM)


def reference(queries, mem_keys, mem_values, grad_out):
    stacked = (split_heads(queries), split_heads(mem_keys), split_heads(mem_values), split_heads(grad_out))
    attended, query_gradients, grad_keys, grad_values = lax.map(one_head, stacked)
    return join_heads(attended), join_heads(query_gradients), join_heads(grad_keys), join_heads(grad_values)
```

```python
import functools
import math

import jax
import jax.numpy as jnp
from jax import lax
from jax.experimental import pallas as pl
from jax.experimental.pallas import tpu as pltpu
from jax.sharding import PartitionSpec as P

HEAD_DIM = 256
MESH = pl.DeviceIdType.MESH
F32 = jnp.float32
BF16 = jnp.bfloat16
NT = (((1,), (1,)), ((), ()))


def kernel(
    sizes,
    q_hbm, k_hbm, v_hbm, o_hbm,
    att_hbm, dq_hbm, gk_ref, gv_ref,
    q_v, o_v, k_v, v_v, kt_v, vt_v, p_v, ds_v, att_v, dq_v,
    part, keep, x_in, z_out, z_in, h_out,
    kv_send, kv_recv, kv_own, qo_sem, out_sem,
    x_send, x_recv, z_send, z_recv, h_send, h_recv,
):
    heads, head_group, outer, rows, mem_rows, share, block = sizes
    memory = mem_rows * head_group
    piece = head_group * share
    me_q, me_h = lax.axis_index("query"), lax.axis_index("head")
    me_hi, me_lo = me_q // 2, me_q % 2
    scale = HEAD_DIM ** -0.5

    def head_peer(step):
        return me_q, lax.rem(me_h + step, head_group)

    def pair_peer():
        return me_hi * 2 + 1 - me_lo, me_h

    def outer_peer(step):
        return lax.rem(me_hi + step, outer) * 2 + me_lo, me_h

    head_steps = [s for s in range(2, head_group)] + [1]

    def kv_copy(j, step, which):
        src, dst = ((k_hbm, k_v), (v_hbm, v_v))[which]
        peer = head_peer(step)
        cols = pl.ds(pl.multiple_of((peer[1] * heads + j) * HEAD_DIM, HEAD_DIM), HEAD_DIM)
        mine = pl.ds(pl.multiple_of(me_h * mem_rows, mem_rows), mem_rows)
        return pltpu.make_async_remote_copy(
            src_ref=src.at[:, cols],
            dst_ref=dst.at[j, mine, :],
            send_sem=kv_send.at[j, step - 1, which],
            recv_sem=kv_recv.at[j, step - 1, which],
            device_id=peer,
            device_id_type=MESH,
        )

    def kv_local(j, which):
        src, dst = ((k_hbm, k_v), (v_hbm, v_v))[which]
        cols = pl.ds(pl.multiple_of((me_h * heads + j) * HEAD_DIM, HEAD_DIM), HEAD_DIM)
        mine = pl.ds(pl.multiple_of(me_h * mem_rows, mem_rows), mem_rows)
        return pltpu.make_async_copy(src.at[:, cols], dst.at[j, mine, :], kv_own.at[j, which])

    def qo_copy(j, which):
        src, dst = ((q_hbm, q_v), (o_hbm, o_v))[which]
        cols = pl.ds(pl.multiple_of(j * HEAD_DIM, HEAD_DIM), HEAD_DIM)
        return pltpu.make_async_copy(src.at[:, cols], dst.at[j], qo_sem.at[j, which])

    def out_copy(j, which):
        src, dst = ((att_v, att_hbm), (dq_v, dq_hbm))[which]
        cols = pl.ds(pl.multiple_of(j * HEAD_DIM, HEAD_DIM), HEAD_DIM)
        return pltpu.make_async_copy(src.at[j], dst.at[:, cols], out_sem.at[j, which])

    def x_copy(j, which):
        return pltpu.make_async_remote_copy(
            src_ref=part.at[j, which],
            dst_ref=x_in.at[j, which],
            send_sem=x_send.at[j, which],
            recv_sem=x_recv.at[j, which],
            device_id=pair_peer(),
            device_id_type=MESH,
        )

    def z_copy(j, step):
        return pltpu.make_async_remote_copy(
            src_ref=z_out.at[j, step - 1],
            dst_ref=z_in.at[j, step - 1],
            send_sem=z_send.at[j, step - 1],
            recv_sem=z_recv.at[j, step - 1],
            device_id=outer_peer(step),
            device_id_type=MESH,
        )

    def h_copy(j, step, which):
        peer = head_peer(step)
        cols = pl.ds(pl.multiple_of((me_h * heads + j) * HEAD_DIM, HEAD_DIM), HEAD_DIM)
        return pltpu.make_async_remote_copy(
            src_ref=h_out.at[j, which, peer[1]],
            dst_ref=(gk_ref, gv_ref)[which].at[:, cols],
            send_sem=h_send.at[j, step - 1, which],
            recv_sem=h_recv.at[j, step - 1, which],
            device_id=peer,
            device_id_type=MESH,
        )

    barrier = pltpu.get_barrier_semaphore()
    peers = [head_peer(s) for s in range(1, head_group)]
    peers += [pair_peer()] + [outer_peer(s) for s in range(1, outer)]
    for peer in peers:
        pl.semaphore_signal(barrier, inc=1, device_id=peer, device_id_type=MESH)
    for which in range(2):
        kv_local(0, which).start()
        qo_copy(0, which).start()
    pl.semaphore_wait(barrier, len(peers))

    def start_inputs(j, carry):
        for step in head_steps:
            for which in range(2):
                kv_copy(j, step, which).start()

        @pl.when(j > 0)
        def _():
            for which in range(2):
                kv_local(j, which).start()
                qo_copy(j, which).start()

        return carry

    lax.fori_loop(0, heads, start_inputs, 0)

    def rows_of(hi, lo):
        return pl.ds(pl.multiple_of((hi * 2 + lo) * piece, piece), piece)

    def work(j):
        for which in range(2):
            kv_local(j, which).wait()
            qo_copy(j, which).wait()
            for step in head_steps:
                kv_copy(j, step, which).wait_recv()
        kt_v[...] = k_v[j].T
        vt_v[...] = v_v[j].T

        def rows_block(r, carry):
            at = pl.ds(pl.multiple_of(r * block, block), block)
            scores = lax.dot_general(k_v[j], q_v[j, at, :], NT, preferred_element_type=F32)
            top = jnp.max(scores, axis=0, keepdims=True)
            weights = jnp.exp2((scores - top) * (scale * math.log2(math.e)))
            probs = (weights * (1.0 / jnp.sum(weights, axis=0, keepdims=True))).astype(BF16)
            p_v[:, at] = probs
            dprobs = lax.dot_general(v_v[j], o_v[j, at, :], NT, preferred_element_type=F32)
            probs32 = probs.astype(F32)
            delta = jnp.sum(probs32 * dprobs, axis=0, keepdims=True)
            dscores = (probs32 * (dprobs - delta)).astype(BF16)
            ds_v[:, at] = dscores
            att = jnp.dot(vt_v[...], probs, preferred_element_type=F32).astype(BF16)
            att_v[j, at, :] = att.T
            dq = (jnp.dot(kt_v[...], dscores, preferred_element_type=F32) * scale).astype(BF16)
            dq_v[j, at, :] = dq.T
            return carry

        lax.fori_loop(0, rows // block, rows_block, 0)
        for which in range(2):
            out_copy(j, which).start()

        for which in (1, 0):
            def piece_block(hi, carry):
                left = (ds_v, p_v)[which]
                right = (q_v, o_v)[which]
                for lo in range(2):
                    total = jnp.dot(
                        left[rows_of(hi, lo), :], right[j], preferred_element_type=F32
                    )
                    if which == 0:
                        total = total * scale

                    @pl.when(me_lo == lo)
                    def _():
                        keep[j, which, hi] = total

                    @pl.when(me_lo != lo)
                    def _():
                        part[j, which, hi] = total.astype(BF16)

                return carry

            lax.fori_loop(0, outer, piece_block, 0)
            x_copy(j, which).start()

    def pair_sum(j):
        for which in range(2):
            x_copy(j, which).wait()
            for step in range(1, outer):
                hi = lax.rem(me_hi + step, outer)
                total = keep[j, which, hi] + x_in[j, which, hi].astype(F32)
                z_out[j, step - 1, which] = total.astype(BF16)
            keep[j, which, me_hi] = keep[j, which, me_hi] + x_in[j, which, me_hi].astype(F32)
        for step in range(1, outer):
            z_copy(j, step).start()

    def outer_sum(j):
        for step in range(1, outer):
            z_copy(j, step).wait()
        for which in range(2):
            total = keep[j, which, me_hi]
            for step in range(1, outer):
                total = total + z_in[j, step - 1, which].astype(F32)
            for h in range(head_group):
                h_out[j, which, h] = total[h * share : (h + 1) * share].astype(BF16)
            for step in head_steps:
                h_copy(j, step, which).start()
            cols = pl.ds(pl.multiple_of((me_h * heads + j) * HEAD_DIM, HEAD_DIM), HEAD_DIM)
            (gk_ref, gv_ref)[which][:, cols] = h_out[j, which, me_h]

    def turn(t, carry):
        @pl.when(t < heads)
        def _():
            work(t)

        @pl.when(jnp.logical_and(t >= 1, t <= heads))
        def _():
            pair_sum(t - 1)

        @pl.when(t >= 2)
        def _():
            outer_sum(t - 2)

        return carry

    lax.fori_loop(0, heads + 2, turn, 0)

    def finish(j, carry):
        for which in range(2):
            out_copy(j, which).wait()
            for step in head_steps:
                kv_copy(j, step, which).wait_send()
                h_copy(j, step, which).wait()
        return carry

    lax.fori_loop(0, heads, finish, 0)


def per_device(queries, mem_keys, mem_values, grad_out):
    head_group = lax.axis_size("head")
    query_group = lax.axis_size("query")
    mem_rows, full_width = mem_keys.shape
    rows, local_width = queries.shape
    heads = local_width // HEAD_DIM
    memory = mem_rows * head_group
    outer = query_group // 2
    share = memory // (query_group * head_group)
    piece = head_group * share
    block = math.gcd(rows, 256)
    sizes = (heads, head_group, outer, rows, mem_rows, share, block)
    big = jax.ShapeDtypeStruct((rows, local_width), BF16)
    small = jax.ShapeDtypeStruct((share, full_width), BF16)
    flops = 12 * rows * memory * local_width
    anywhere = pl.BlockSpec(memory_space=pl.ANY)
    vmem = pl.BlockSpec(memory_space=pltpu.VMEM)
    dma = pltpu.SemaphoreType.DMA
    return tuple(pl.pallas_call(
        functools.partial(kernel, sizes),
        out_shape=(big, big, small, small),
        in_specs=[anywhere] * 4,
        out_specs=(anywhere, anywhere, vmem, vmem),
        scratch_shapes=[
            pltpu.VMEM((heads, rows, HEAD_DIM), BF16),
            pltpu.VMEM((heads, rows, HEAD_DIM), BF16),
            pltpu.VMEM((heads, memory, HEAD_DIM), BF16),
            pltpu.VMEM((heads, memory, HEAD_DIM), BF16),
            pltpu.VMEM((HEAD_DIM, memory), BF16),
            pltpu.VMEM((HEAD_DIM, memory), BF16),
            pltpu.VMEM((memory, rows), BF16),
            pltpu.VMEM((memory, rows), BF16),
            pltpu.VMEM((heads, rows, HEAD_DIM), BF16),
            pltpu.VMEM((heads, rows, HEAD_DIM), BF16),
            pltpu.VMEM((heads, 2, outer, piece, HEAD_DIM), BF16),
            pltpu.VMEM((heads, 2, outer, piece, HEAD_DIM), F32),
            pltpu.VMEM((heads, 2, outer, piece, HEAD_DIM), BF16),
            pltpu.VMEM((heads, outer - 1, 2, piece, HEAD_DIM), BF16),
            pltpu.VMEM((heads, outer - 1, 2, piece, HEAD_DIM), BF16),
            pltpu.VMEM((heads, 2, head_group, share, HEAD_DIM), BF16),
            dma((heads, head_group - 1, 2)),
            dma((heads, head_group - 1, 2)),
            dma((heads, 2)),
            dma((heads, 2)),
            dma((heads, 2)),
            dma((heads, 2)),
            dma((heads, 2)),
            dma((heads, outer - 1)),
            dma((heads, outer - 1)),
            dma((heads, head_group - 1, 2)),
            dma((heads, head_group - 1, 2)),
        ],
        compiler_params=pltpu.CompilerParams(
            collective_id=0, has_side_effects=True, vmem_limit_bytes=56 * 1024 * 1024
        ),
        cost_estimate=pl.CostEstimate(
            flops=flops,
            bytes_accessed=8 * rows * local_width + 4 * mem_rows * full_width,
            transcendentals=rows * memory * heads,
        ),
    )(queries, mem_keys, mem_values, grad_out))


def solution(mesh):
    in_specs = (P("query", "head"), P("head", None), P("head", None), P("query", "head"))
    out_specs = (
        P("query", "head"),
        P("query", "head"),
        P(("query", "head"), None),
        P(("query", "head"), None),
    )
    return jax.shard_map(
        per_device, mesh=mesh, in_specs=in_specs, out_specs=out_specs, check_vma=False
    )
```

```python
import functools
import math

import jax
import jax.numpy as jnp
from jax import lax
from jax.experimental import pallas as pl
from jax.experimental.pallas import tpu as pltpu
from jax.sharding import PartitionSpec as P

HEAD_DIM = 256
MESH = pl.DeviceIdType.MESH
F32 = jnp.float32
BF16 = jnp.bfloat16
NT = (((1,), (1,)), ((), ()))


def kernel(
    sizes,
    q_hbm, k_hbm, v_hbm, o_hbm,
    att_hbm, dq_hbm, gk_ref, gv_ref,
    q_v, o_v, k_v, v_v, kt_v, vt_v, p_v, ds_v, att_v, dq_v,
    part, keep, x_in, z_out, z_in, h_out,
    kv_send, kv_recv, kv_own, qo_sem, out_sem,
    x_send, x_recv, z_send, z_recv, h_send, h_recv,
):
    heads, head_group, outer, rows, mem_rows, share, block = sizes
    memory = mem_rows * head_group
    piece = head_group * share
    me_q, me_h = lax.axis_index("query"), lax.axis_index("head")
    me_hi, me_lo = me_q // 2, me_q % 2
    scale = HEAD_DIM ** -0.5

    def head_peer(step):
        return me_q, lax.rem(me_h + step, head_group)

    def pair_peer():
        return me_hi * 2 + 1 - me_lo, me_h

    def outer_peer(step):
        return lax.rem(me_hi + step, outer) * 2 + me_lo, me_h

    head_steps = [s for s in range(2, head_group)] + [1]

    def kv_copy(j, step, which):
        src, dst = ((k_hbm, k_v), (v_hbm, v_v))[which]
        peer = head_peer(step)
        cols = pl.ds(pl.multiple_of((peer[1] * heads + j) * HEAD_DIM, HEAD_DIM), HEAD_DIM)
        mine = pl.ds(pl.multiple_of(me_h * mem_rows, mem_rows), mem_rows)
        return pltpu.make_async_remote_copy(
            src_ref=src.at[:, cols],
            dst_ref=dst.at[j, mine, :],
            send_sem=kv_send.at[j, step - 1, which],
            recv_sem=kv_recv.at[j, step - 1, which],
            device_id=peer,
            device_id_type=MESH,
        )

    def kv_local(j, which):
        src, dst = ((k_hbm, k_v), (v_hbm, v_v))[which]
        cols = pl.ds(pl.multiple_of((me_h * heads + j) * HEAD_DIM, HEAD_DIM), HEAD_DIM)
        mine = pl.ds(pl.multiple_of(me_h * mem_rows, mem_rows), mem_rows)
        return pltpu.make_async_copy(src.at[:, cols], dst.at[j, mine, :], kv_own.at[j, which])

    def qo_copy(j, which):
        src, dst = ((q_hbm, q_v), (o_hbm, o_v))[which]
        cols = pl.ds(pl.multiple_of(j * HEAD_DIM, HEAD_DIM), HEAD_DIM)
        return pltpu.make_async_copy(src.at[:, cols], dst.at[j], qo_sem.at[j, which])

    def out_copy(j, which):
        src, dst = ((att_v, att_hbm), (dq_v, dq_hbm))[which]
        cols = pl.ds(pl.multiple_of(j * HEAD_DIM, HEAD_DIM), HEAD_DIM)
        return pltpu.make_async_copy(src.at[j], dst.at[:, cols], out_sem.at[j, which])

    def x_copy(j, which):
        return pltpu.make_async_remote_copy(
            src_ref=part.at[j, which],
            dst_ref=x_in.at[j, which],
            send_sem=x_send.at[j, which],
            recv_sem=x_recv.at[j, which],
            device_id=pair_peer(),
            device_id_type=MESH,
        )

    def z_copy(j, step):
        return pltpu.make_async_remote_copy(
            src_ref=z_out.at[j, step - 1],
            dst_ref=z_in.at[j, step - 1],
            send_sem=z_send.at[j, step - 1],
            recv_sem=z_recv.at[j, step - 1],
            device_id=outer_peer(step),
            device_id_type=MESH,
        )

    def h_copy(j, step, which):
        peer = head_peer(step)
        cols = pl.ds(pl.multiple_of((me_h * heads + j) * HEAD_DIM, HEAD_DIM), HEAD_DIM)
        return pltpu.make_async_remote_copy(
            src_ref=h_out.at[j, which, peer[1]],
            dst_ref=(gk_ref, gv_ref)[which].at[:, cols],
            send_sem=h_send.at[j, step - 1, which],
            recv_sem=h_recv.at[j, step - 1, which],
            device_id=peer,
            device_id_type=MESH,
        )

    barrier = pltpu.get_barrier_semaphore()
    peers = [head_peer(s) for s in range(1, head_group)]
    peers += [pair_peer()] + [outer_peer(s) for s in range(1, outer)]
    for peer in peers:
        pl.semaphore_signal(barrier, inc=1, device_id=peer, device_id_type=MESH)
    for which in range(2):
        kv_local(0, which).start()
        qo_copy(0, which).start()
    pl.semaphore_wait(barrier, len(peers))

    def start_inputs(j, carry):
        for step in head_steps:
            for which in range(2):
                kv_copy(j, step, which).start()

        @pl.when(j > 0)
        def _():
            for which in range(2):
                kv_local(j, which).start()
                qo_copy(j, which).start()

        return carry

    lax.fori_loop(0, heads, start_inputs, 0)

    def work(j):
        for which in range(2):
            kv_local(j, which).wait()
            qo_copy(j, which).wait()
            for step in head_steps:
                kv_copy(j, step, which).wait_recv()
        kt_v[...] = k_v[j].T
        vt_v[...] = v_v[j].T

        def products(r):
            at = slice(r * block, (r + 1) * block)
            scores = lax.dot_general(k_v[j], q_v[j, at, :], NT, preferred_element_type=F32)
            dprobs = lax.dot_general(v_v[j], o_v[j, at, :], NT, preferred_element_type=F32)
            return scores, dprobs

        blocks = rows // block
        ahead = products(0)
        for r in range(blocks):
            scores, dprobs = ahead
            if r + 1 < blocks:
                ahead = products(r + 1)
            at = slice(r * block, (r + 1) * block)
            top = jnp.max(scores, axis=0, keepdims=True)
            weights = jnp.exp2((scores - top) * (scale * math.log2(math.e)))
            probs = (weights * (1.0 / jnp.sum(weights, axis=0, keepdims=True))).astype(BF16)
            p_v[:, at] = probs
            probs32 = probs.astype(F32)
            delta = jnp.sum(probs32 * dprobs, axis=0, keepdims=True)
            dscores = (probs32 * (dprobs - delta)).astype(BF16)
            ds_v[:, at] = dscores
            att = jnp.dot(vt_v[...], probs, preferred_element_type=F32).astype(BF16)
            att_v[j, at, :] = att.T
            dq = (jnp.dot(kt_v[...], dscores, preferred_element_type=F32) * scale).astype(BF16)
            dq_v[j, at, :] = dq.T

        for which in range(2):
            out_copy(j, which).start()

        for which in (1, 0):
            left = (ds_v, p_v)[which]
            right = (q_v, o_v)[which]
            total = jnp.dot(left[...], right[j], preferred_element_type=F32)
            if which == 0:
                total = total * scale
            keep[j, which] = total.reshape(outer, 2, piece, HEAD_DIM)
            part[j, which] = keep[j, which, :, 1 - me_lo].astype(BF16)
            x_copy(j, which).start()

    def pair_sum(j):
        for which in range(2):
            x_copy(j, which).wait()
            for step in range(1, outer):
                hi = lax.rem(me_hi + step, outer)
                total = keep[j, which, hi, me_lo] + x_in[j, which, hi].astype(F32)
                z_out[j, step - 1, which] = total.astype(BF16)
            keep[j, which, me_hi, me_lo] += x_in[j, which, me_hi].astype(F32)
        for step in range(1, outer):
            z_copy(j, step).start()

    def outer_sum(j):
        for step in range(1, outer):
            z_copy(j, step).wait()
        for which in range(2):
            total = keep[j, which, me_hi, me_lo]
            for step in range(1, outer):
                total = total + z_in[j, step - 1, which].astype(F32)
            for h in range(head_group):
                h_out[j, which, h] = total[h * share : (h + 1) * share].astype(BF16)
            for step in head_steps:
                h_copy(j, step, which).start()
            cols = pl.ds(pl.multiple_of((me_h * heads + j) * HEAD_DIM, HEAD_DIM), HEAD_DIM)
            (gk_ref, gv_ref)[which][:, cols] = h_out[j, which, me_h]

    def turn(t, carry):
        @pl.when(t < heads)
        def _():
            work(t)

        @pl.when(jnp.logical_and(t >= 1, t <= heads))
        def _():
            pair_sum(t - 1)

        @pl.when(t >= 2)
        def _():
            outer_sum(t - 2)

        return carry

    lax.fori_loop(0, heads + 2, turn, 0)

    def finish(j, carry):
        for which in range(2):
            out_copy(j, which).wait()
            for step in head_steps:
                kv_copy(j, step, which).wait_send()
                h_copy(j, step, which).wait()
        return carry

    lax.fori_loop(0, heads, finish, 0)


def per_device(queries, mem_keys, mem_values, grad_out):
    head_group = lax.axis_size("head")
    query_group = lax.axis_size("query")
    mem_rows, full_width = mem_keys.shape
    rows, local_width = queries.shape
    heads = local_width // HEAD_DIM
    memory = mem_rows * head_group
    outer = query_group // 2
    share = memory // (query_group * head_group)
    piece = head_group * share
    block = math.gcd(rows, 256)
    sizes = (heads, head_group, outer, rows, mem_rows, share, block)
    big = jax.ShapeDtypeStruct((rows, local_width), BF16)
    small = jax.ShapeDtypeStruct((share, full_width), BF16)
    flops = 12 * rows * memory * local_width
    anywhere = pl.BlockSpec(memory_space=pl.ANY)
    vmem = pl.BlockSpec(memory_space=pltpu.VMEM)
    dma = pltpu.SemaphoreType.DMA
    return tuple(pl.pallas_call(
        functools.partial(kernel, sizes),
        out_shape=(big, big, small, small),
        in_specs=[anywhere] * 4,
        out_specs=(anywhere, anywhere, vmem, vmem),
        scratch_shapes=[
            pltpu.VMEM((heads, rows, HEAD_DIM), BF16),
            pltpu.VMEM((heads, rows, HEAD_DIM), BF16),
            pltpu.VMEM((heads, memory, HEAD_DIM), BF16),
            pltpu.VMEM((heads, memory, HEAD_DIM), BF16),
            pltpu.VMEM((HEAD_DIM, memory), BF16),
            pltpu.VMEM((HEAD_DIM, memory), BF16),
            pltpu.VMEM((memory, rows), BF16),
            pltpu.VMEM((memory, rows), BF16),
            pltpu.VMEM((heads, rows, HEAD_DIM), BF16),
            pltpu.VMEM((heads, rows, HEAD_DIM), BF16),
            pltpu.VMEM((heads, 2, outer, piece, HEAD_DIM), BF16),
            pltpu.VMEM((heads, 2, outer, 2, piece, HEAD_DIM), F32),
            pltpu.VMEM((heads, 2, outer, piece, HEAD_DIM), BF16),
            pltpu.VMEM((heads, outer - 1, 2, piece, HEAD_DIM), BF16),
            pltpu.VMEM((heads, outer - 1, 2, piece, HEAD_DIM), BF16),
            pltpu.VMEM((heads, 2, head_group, share, HEAD_DIM), BF16),
            dma((heads, head_group - 1, 2)),
            dma((heads, head_group - 1, 2)),
            dma((heads, 2)),
            dma((heads, 2)),
            dma((heads, 2)),
            dma((heads, 2)),
            dma((heads, 2)),
            dma((heads, outer - 1)),
            dma((heads, outer - 1)),
            dma((heads, head_group - 1, 2)),
            dma((heads, head_group - 1, 2)),
        ],
        compiler_params=pltpu.CompilerParams(
            collective_id=0, has_side_effects=True, vmem_limit_bytes=56 * 1024 * 1024
        ),
        cost_estimate=pl.CostEstimate(
            flops=flops,
            bytes_accessed=8 * rows * local_width + 4 * mem_rows * full_width,
            transcendentals=rows * memory * heads,
        ),
    )(queries, mem_keys, mem_values, grad_out))


def solution(mesh):
    in_specs = (P("query", "head"), P("head", None), P("head", None), P("query", "head"))
    out_specs = (
        P("query", "head"),
        P("query", "head"),
        P(("query", "head"), None),
        P(("query", "head"), None),
    )
    return jax.shard_map(
        per_device, mesh=mesh, in_specs=in_specs, out_specs=out_specs, check_vma=False
    )
```

```python
import functools
import math

import jax
import jax.numpy as jnp
from jax import lax
from jax.experimental import pallas as pl
from jax.experimental.pallas import tpu as pltpu
from jax.sharding import PartitionSpec as P

HEAD_DIM = 256
MESH = pl.DeviceIdType.MESH
F32 = jnp.float32
BF16 = jnp.bfloat16
NT = (((1,), (1,)), ((), ()))


def kernel(
    sizes,
    q_hbm, k_hbm, v_hbm, o_hbm,
    att_hbm, dq_hbm, gk_ref, gv_ref,
    q_v, o_v, k_v, v_v, kt_v, vt_v, p_v, ds_v, att_v, dq_v,
    part, keep, x_in, z_out, z_in, h_out,
    kv_send, kv_recv, kv_own, qo_sem, out_sem,
    x_send, x_recv, z_send, z_recv, h_send, h_recv,
):
    heads, head_group, outer, rows, mem_rows, share, block = sizes
    memory = mem_rows * head_group
    piece = head_group * share
    me_q, me_h = lax.axis_index("query"), lax.axis_index("head")
    me_hi, me_lo = me_q // 2, me_q % 2
    scale = HEAD_DIM ** -0.5

    def head_peer(step):
        return me_q, lax.rem(me_h + step, head_group)

    def pair_peer():
        return me_hi * 2 + 1 - me_lo, me_h

    def outer_peer(step):
        return lax.rem(me_hi + step, outer) * 2 + me_lo, me_h

    head_steps = [s for s in range(2, head_group)] + [1]

    def kv_copy(j, step, which):
        src, dst = ((k_hbm, k_v), (v_hbm, v_v))[which]
        peer = head_peer(step)
        cols = pl.ds(pl.multiple_of((peer[1] * heads + j) * HEAD_DIM, HEAD_DIM), HEAD_DIM)
        mine = pl.ds(pl.multiple_of(me_h * mem_rows, mem_rows), mem_rows)
        return pltpu.make_async_remote_copy(
            src_ref=src.at[:, cols],
            dst_ref=dst.at[j, mine, :],
            send_sem=kv_send.at[j, step - 1, which],
            recv_sem=kv_recv.at[j, step - 1, which],
            device_id=peer,
            device_id_type=MESH,
        )

    def kv_local(j, which):
        src, dst = ((k_hbm, k_v), (v_hbm, v_v))[which]
        cols = pl.ds(pl.multiple_of((me_h * heads + j) * HEAD_DIM, HEAD_DIM), HEAD_DIM)
        mine = pl.ds(pl.multiple_of(me_h * mem_rows, mem_rows), mem_rows)
        return pltpu.make_async_copy(src.at[:, cols], dst.at[j, mine, :], kv_own.at[j, which])

    def qo_copy(j, which):
        src, dst = ((q_hbm, q_v), (o_hbm, o_v))[which]
        cols = pl.ds(pl.multiple_of(j * HEAD_DIM, HEAD_DIM), HEAD_DIM)
        return pltpu.make_async_copy(src.at[:, cols], dst.at[j], qo_sem.at[j, which])

    def out_copy(j, which):
        src, dst = ((att_v, att_hbm), (dq_v, dq_hbm))[which]
        cols = pl.ds(pl.multiple_of(j * HEAD_DIM, HEAD_DIM), HEAD_DIM)
        return pltpu.make_async_copy(src.at[j], dst.at[:, cols], out_sem.at[j, which])

    def x_copy(j, which):
        return pltpu.make_async_remote_copy(
            src_ref=part.at[j, which],
            dst_ref=x_in.at[j, which],
            send_sem=x_send.at[j, which],
            recv_sem=x_recv.at[j, which],
            device_id=pair_peer(),
            device_id_type=MESH,
        )

    def z_copy(j, step, which):
        return pltpu.make_async_remote_copy(
            src_ref=z_out.at[j, step - 1, which],
            dst_ref=z_in.at[j, step - 1, which],
            send_sem=z_send.at[j, step - 1, which],
            recv_sem=z_recv.at[j, step - 1, which],
            device_id=outer_peer(step),
            device_id_type=MESH,
        )

    def h_copy(j, step, which):
        peer = head_peer(step)
        cols = pl.ds(pl.multiple_of((me_h * heads + j) * HEAD_DIM, HEAD_DIM), HEAD_DIM)
        return pltpu.make_async_remote_copy(
            src_ref=h_out.at[j, which, peer[1]],
            dst_ref=(gk_ref, gv_ref)[which].at[:, cols],
            send_sem=h_send.at[j, step - 1, which],
            recv_sem=h_recv.at[j, step - 1, which],
            device_id=peer,
            device_id_type=MESH,
        )

    barrier = pltpu.get_barrier_semaphore()
    peers = [head_peer(s) for s in range(1, head_group)]
    peers += [pair_peer()] + [outer_peer(s) for s in range(1, outer)]
    for peer in peers:
        pl.semaphore_signal(barrier, inc=1, device_id=peer, device_id_type=MESH)
    for which in range(2):
        kv_local(0, which).start()
        qo_copy(0, which).start()
    pl.semaphore_wait(barrier, len(peers))

    def send_inputs(j):
        for step in head_steps:
            for which in range(2):
                kv_copy(j, step, which).start()

    def inputs_sent(j):
        for step in head_steps:
            for which in range(2):
                kv_copy(j, step, which).wait_send()

    send_inputs(0)

    def start_local(j, carry):
        for which in range(2):
            kv_local(j, which).start()
            qo_copy(j, which).start()
        return carry

    lax.fori_loop(1, heads, start_local, 0)
    inputs_sent(0)
    if heads > 1:
        send_inputs(1)

    def work(j):
        for which in range(2):
            kv_local(j, which).wait()
            qo_copy(j, which).wait()
            for step in head_steps:
                kv_copy(j, step, which).wait_recv()
        kt_v[...] = k_v[j].T
        vt_v[...] = v_v[j].T

        def products(r):
            at = slice(r * block, (r + 1) * block)
            scores = lax.dot_general(k_v[j], q_v[j, at, :], NT, preferred_element_type=F32)
            dprobs = lax.dot_general(v_v[j], o_v[j, at, :], NT, preferred_element_type=F32)
            return scores, dprobs

        blocks = rows // block
        ahead = products(0)
        for r in range(blocks):
            scores, dprobs = ahead
            if r + 1 < blocks:
                ahead = products(r + 1)
            at = slice(r * block, (r + 1) * block)
            top = jnp.max(scores, axis=0, keepdims=True)
            weights = jnp.exp2((scores - top) * (scale * math.log2(math.e)))
            probs = (weights * (1.0 / jnp.sum(weights, axis=0, keepdims=True))).astype(BF16)
            p_v[:, at] = probs
            probs32 = probs.astype(F32)
            delta = jnp.sum(probs32 * dprobs, axis=0, keepdims=True)
            dscores = (probs32 * (dprobs - delta)).astype(BF16)
            ds_v[:, at] = dscores
            att = jnp.dot(vt_v[...], probs, preferred_element_type=F32).astype(BF16)
            att_v[j, at, :] = att.T
            dq = (jnp.dot(kt_v[...], dscores, preferred_element_type=F32) * scale).astype(BF16)
            dq_v[j, at, :] = dq.T

        for which in range(2):
            out_copy(j, which).start()

        for which in (1, 0):
            left = (ds_v, p_v)[which]
            right = (q_v, o_v)[which]
            total = jnp.dot(left[...], right[j], preferred_element_type=F32)
            if which == 0:
                total = total * scale
            keep[j, which] = total.reshape(outer, 2, piece, HEAD_DIM)
            part[j, which] = keep[j, which, :, 1 - me_lo].astype(BF16)
            x_copy(j, which).start()

        @pl.when(j + 1 < heads)
        def _():
            inputs_sent(j + 1)

        @pl.when(j + 2 < heads)
        def _():
            send_inputs(j + 2)

    def pair_sum(j):
        for which in (1, 0):
            x_copy(j, which).wait()
            for step in range(1, outer):
                hi = lax.rem(me_hi + step, outer)
                total = keep[j, which, hi, me_lo] + x_in[j, which, hi].astype(F32)
                z_out[j, step - 1, which] = total.astype(BF16)
                z_copy(j, step, which).start()
            keep[j, which, me_hi, me_lo] += x_in[j, which, me_hi].astype(F32)

    def outer_sum(j):
        for which in (1, 0):
            for step in range(1, outer):
                z_copy(j, step, which).wait()
            total = keep[j, which, me_hi, me_lo]
            for step in range(1, outer):
                total = total + z_in[j, step - 1, which].astype(F32)
            for h in range(head_group):
                h_out[j, which, h] = total[h * share : (h + 1) * share].astype(BF16)
            for step in head_steps:
                h_copy(j, step, which).start()
            cols = pl.ds(pl.multiple_of((me_h * heads + j) * HEAD_DIM, HEAD_DIM), HEAD_DIM)
            (gk_ref, gv_ref)[which][:, cols] = h_out[j, which, me_h]

    def turn(t, carry):
        @pl.when(t < heads)
        def _():
            work(t)

        @pl.when(jnp.logical_and(t >= 1, t <= heads))
        def _():
            pair_sum(t - 1)

        @pl.when(t >= 2)
        def _():
            outer_sum(t - 2)

        return carry

    lax.fori_loop(0, heads + 2, turn, 0)

    def finish(j, carry):
        for which in range(2):
            out_copy(j, which).wait()
            for step in head_steps:
                h_copy(j, step, which).wait()
        return carry

    lax.fori_loop(0, heads, finish, 0)


def per_device(queries, mem_keys, mem_values, grad_out):
    head_group = lax.axis_size("head")
    query_group = lax.axis_size("query")
    mem_rows, full_width = mem_keys.shape
    rows, local_width = queries.shape
    heads = local_width // HEAD_DIM
    memory = mem_rows * head_group
    outer = query_group // 2
    share = memory // (query_group * head_group)
    piece = head_group * share
    block = math.gcd(rows, 256)
    sizes = (heads, head_group, outer, rows, mem_rows, share, block)
    big = jax.ShapeDtypeStruct((rows, local_width), BF16)
    small = jax.ShapeDtypeStruct((share, full_width), BF16)
    flops = 12 * rows * memory * local_width
    anywhere = pl.BlockSpec(memory_space=pl.ANY)
    vmem = pl.BlockSpec(memory_space=pltpu.VMEM)
    dma = pltpu.SemaphoreType.DMA
    return tuple(pl.pallas_call(
        functools.partial(kernel, sizes),
        out_shape=(big, big, small, small),
        in_specs=[pl.BlockSpec(memory_space=pltpu.HBM)] * 4,
        out_specs=(anywhere, anywhere, vmem, vmem),
        scratch_shapes=[
            pltpu.VMEM((heads, rows, HEAD_DIM), BF16),
            pltpu.VMEM((heads, rows, HEAD_DIM), BF16),
            pltpu.VMEM((heads, memory, HEAD_DIM), BF16),
            pltpu.VMEM((heads, memory, HEAD_DIM), BF16),
            pltpu.VMEM((HEAD_DIM, memory), BF16),
            pltpu.VMEM((HEAD_DIM, memory), BF16),
            pltpu.VMEM((memory, rows), BF16),
            pltpu.VMEM((memory, rows), BF16),
            pltpu.VMEM((heads, rows, HEAD_DIM), BF16),
            pltpu.VMEM((heads, rows, HEAD_DIM), BF16),
            pltpu.VMEM((heads, 2, outer, piece, HEAD_DIM), BF16),
            pltpu.VMEM((heads, 2, outer, 2, piece, HEAD_DIM), F32),
            pltpu.VMEM((heads, 2, outer, piece, HEAD_DIM), BF16),
            pltpu.VMEM((heads, outer - 1, 2, piece, HEAD_DIM), BF16),
            pltpu.VMEM((heads, outer - 1, 2, piece, HEAD_DIM), BF16),
            pltpu.VMEM((heads, 2, head_group, share, HEAD_DIM), BF16),
            dma((heads, head_group - 1, 2)),
            dma((heads, head_group - 1, 2)),
            dma((heads, 2)),
            dma((heads, 2)),
            dma((heads, 2)),
            dma((heads, 2)),
            dma((heads, 2)),
            dma((heads, outer - 1, 2)),
            dma((heads, outer - 1, 2)),
            dma((heads, head_group - 1, 2)),
            dma((heads, head_group - 1, 2)),
        ],
        compiler_params=pltpu.CompilerParams(
            collective_id=0, has_side_effects=True, vmem_limit_bytes=46 * 1024 * 1024
        ),
        cost_estimate=pl.CostEstimate(
            flops=flops,
            bytes_accessed=8 * rows * local_width + 4 * mem_rows * full_width,
            transcendentals=rows * memory * heads,
        ),
    )(queries, mem_keys, mem_values, grad_out))


def solution(mesh):
    in_specs = (P("query", "head"), P("head", None), P("head", None), P("query", "head"))
    out_specs = (
        P("query", "head"),
        P("query", "head"),
        P(("query", "head"), None),
        P(("query", "head"), None),
    )
    return jax.shard_map(
        per_device, mesh=mesh, in_specs=in_specs, out_specs=out_specs, check_vma=False
    )
```

```python
import functools
import math

import jax
import jax.numpy as jnp
from jax import lax
from jax.experimental import pallas as pl
from jax.experimental.pallas import tpu as pltpu
from jax.sharding import PartitionSpec as P

HEAD_DIM = 256
MESH = pl.DeviceIdType.MESH
F32 = jnp.float32
BF16 = jnp.bfloat16
NT = (((1,), (1,)), ((), ()))


def kernel(
    sizes,
    q_hbm, k_hbm, v_hbm, o_hbm,
    att_hbm, dq_hbm, gk_ref, gv_ref,
    q_v, o_v, k_v, v_v, kt_v, vt_v, p_v, ds_v, att_v, dq_v,
    part, keep, x_in, z_out, z_in, h_out,
    kv_send, kv_recv, forward_send, kv_own, qo_sem, out_sem,
    x_send, x_recv, z_send, z_recv, h_send, h_recv,
):
    heads, head_group, outer, rows, mem_rows, share, block = sizes
    memory = mem_rows * head_group
    piece = head_group * share
    me_q, me_h = lax.axis_index("query"), lax.axis_index("head")
    me_hi, me_lo = me_q // 2, me_q % 2
    scale = HEAD_DIM ** -0.5

    def head_peer(step):
        return me_q, lax.rem(me_h + step, head_group)

    def pair_peer():
        return me_hi * 2 + 1 - me_lo, me_h

    def near_peer():
        return (me_hi + 1 - 2 * parity) * 2 + me_lo, me_h

    def outer_peer(step):
        return lax.rem(me_hi + step, outer) * 2 + me_lo, me_h

    head_steps = range(1, head_group)
    parity = me_hi % 2

    def kv_copy(j, step, which):
        src, dst = ((k_hbm, k_v), (v_hbm, v_v))[which]
        peer = head_peer(step)
        cols = pl.ds(pl.multiple_of((peer[1] * heads + j) * HEAD_DIM, HEAD_DIM), HEAD_DIM)
        mine = pl.ds(pl.multiple_of(me_h * mem_rows, mem_rows), mem_rows)
        return pltpu.make_async_remote_copy(
            src_ref=src.at[:, cols],
            dst_ref=dst.at[j, mine, :],
            send_sem=kv_send.at[j, step - 1, which],
            recv_sem=kv_recv.at[j, step - 1, which],
            device_id=peer,
            device_id_type=MESH,
        )

    def sends(step):
        same = head_peer(step)[1] // 2 == me_h // 2
        return jnp.logical_or(same, me_h % 2 == parity)

    def forwards(step):
        source = lax.rem(me_h + head_group - step, head_group)
        return jnp.logical_and(source // 2 != me_h // 2, source % 2 == parity)

    def kv_forward(j, step, which):
        source = lax.rem(me_h + head_group - step, head_group)
        block_rows = pl.ds(pl.multiple_of(source * mem_rows, mem_rows), mem_rows)
        buffer = (k_v, v_v)[which].at[j, block_rows, :]
        return pltpu.make_async_remote_copy(
            src_ref=buffer,
            dst_ref=buffer,
            send_sem=forward_send.at[j, step - 1, which],
            recv_sem=kv_recv.at[j, step - 1, which],
            device_id=near_peer(),
            device_id_type=MESH,
        )

    def kv_local(j, which):
        src, dst = ((k_hbm, k_v), (v_hbm, v_v))[which]
        cols = pl.ds(pl.multiple_of((me_h * heads + j) * HEAD_DIM, HEAD_DIM), HEAD_DIM)
        mine = pl.ds(pl.multiple_of(me_h * mem_rows, mem_rows), mem_rows)
        return pltpu.make_async_copy(src.at[:, cols], dst.at[j, mine, :], kv_own.at[j, which])

    def qo_copy(j, which):
        src, dst = ((q_hbm, q_v), (o_hbm, o_v))[which]
        cols = pl.ds(pl.multiple_of(j * HEAD_DIM, HEAD_DIM), HEAD_DIM)
        return pltpu.make_async_copy(src.at[:, cols], dst.at[j], qo_sem.at[j, which])

    def out_copy(j, which):
        src, dst = ((att_v, att_hbm), (dq_v, dq_hbm))[which]
        cols = pl.ds(pl.multiple_of(j * HEAD_DIM, HEAD_DIM), HEAD_DIM)
        return pltpu.make_async_copy(src.at[j], dst.at[:, cols], out_sem.at[j, which])

    def x_copy(j, which):
        return pltpu.make_async_remote_copy(
            src_ref=part.at[j, which],
            dst_ref=x_in.at[j, which],
            send_sem=x_send.at[j, which],
            recv_sem=x_recv.at[j, which],
            device_id=pair_peer(),
            device_id_type=MESH,
        )

    def z_copy(j, step, which):
        return pltpu.make_async_remote_copy(
            src_ref=z_out.at[j, step - 1, which],
            dst_ref=z_in.at[j, step - 1, which],
            send_sem=z_send.at[j, step - 1, which],
            recv_sem=z_recv.at[j, step - 1, which],
            device_id=outer_peer(step),
            device_id_type=MESH,
        )

    def h_copy(j, step, which):
        peer = head_peer(step)
        cols = pl.ds(pl.multiple_of((me_h * heads + j) * HEAD_DIM, HEAD_DIM), HEAD_DIM)
        return pltpu.make_async_remote_copy(
            src_ref=h_out.at[j, which, peer[1]],
            dst_ref=(gk_ref, gv_ref)[which].at[:, cols],
            send_sem=h_send.at[j, step - 1, which],
            recv_sem=h_recv.at[j, step - 1, which],
            device_id=peer,
            device_id_type=MESH,
        )

    barrier = pltpu.get_barrier_semaphore()
    peers = [head_peer(s) for s in range(1, head_group)]
    peers += [pair_peer()] + [outer_peer(s) for s in range(1, outer)]
    for peer in peers:
        pl.semaphore_signal(barrier, inc=1, device_id=peer, device_id_type=MESH)
    for which in range(2):
        kv_local(0, which).start()
        qo_copy(0, which).start()
    pl.semaphore_wait(barrier, len(peers))

    def send_inputs(j):
        for step in head_steps:
            @pl.when(sends(step))
            def _():
                for which in range(2):
                    kv_copy(j, step, which).start()

    def inputs_sent(j):
        for step in head_steps:
            @pl.when(sends(step))
            def _():
                for which in range(2):
                    kv_copy(j, step, which).wait_send()

    def forward_inputs(j):
        for step in head_steps:
            @pl.when(forwards(step))
            def _():
                for which in range(2):
                    kv_copy(j, step, which).wait_recv()
                    kv_forward(j, step, which).start()

    def inputs_here(j):
        for step in head_steps:
            @pl.when(jnp.logical_not(forwards(step)))
            def _():
                for which in range(2):
                    kv_copy(j, step, which).wait_recv()

    def forwards_sent(j):
        for step in head_steps:
            @pl.when(forwards(step))
            def _():
                for which in range(2):
                    kv_forward(j, step, which).wait_send()

    def advance(j):
        inputs_sent(j)

        @pl.when(j + 1 < heads)
        def _():
            send_inputs(j + 1)

        forward_inputs(j)

    send_inputs(0)

    def start_local(j, carry):
        for which in range(2):
            kv_local(j, which).start()
            qo_copy(j, which).start()
        return carry

    lax.fori_loop(1, heads, start_local, 0)
    advance(0)

    def pair_sum(j):
        for which in (1, 0):
            x_copy(j, which).wait()
            for step in range(1, outer):
                hi = lax.rem(me_hi + step, outer)
                total = keep[j, which, hi, me_lo] + x_in[j, which, hi].astype(F32)
                z_out[j, step - 1, which] = total.astype(BF16)
                z_copy(j, step, which).start()
            keep[j, which, me_hi, me_lo] += x_in[j, which, me_hi].astype(F32)

    def work(j):
        for which in range(2):
            kv_local(j, which).wait()
            qo_copy(j, which).wait()
        inputs_here(j)
        kt_v[...] = k_v[j].T
        vt_v[...] = v_v[j].T

        def products(r):
            at = slice(r * block, (r + 1) * block)
            scores = lax.dot_general(k_v[j], q_v[j, at, :], NT, preferred_element_type=F32)
            dprobs = lax.dot_general(v_v[j], o_v[j, at, :], NT, preferred_element_type=F32)
            return scores, dprobs

        blocks = rows // block
        ahead = products(0)
        for r in range(blocks):
            scores, dprobs = ahead
            if r + 1 < blocks:
                ahead = products(r + 1)
            if r == 1:
                @pl.when(j + 1 < heads)
                def _():
                    advance(j + 1)

            at = slice(r * block, (r + 1) * block)
            top = jnp.max(scores, axis=0, keepdims=True)
            weights = jnp.exp2((scores - top) * (scale * math.log2(math.e)))
            probs = (weights * (1.0 / jnp.sum(weights, axis=0, keepdims=True))).astype(BF16)
            p_v[:, at] = probs
            probs32 = probs.astype(F32)
            delta = jnp.sum(probs32 * dprobs, axis=0, keepdims=True)
            dscores = (probs32 * (dprobs - delta)).astype(BF16)
            ds_v[:, at] = dscores
            att = jnp.dot(vt_v[...], probs, preferred_element_type=F32).astype(BF16)
            att_v[j, at, :] = att.T
            dq = jnp.dot(kt_v[...], dscores, preferred_element_type=F32).astype(BF16)
            dq_v[j, at, :] = dq.T

        for which in range(2):
            out_copy(j, which).start()

        for which in (1, 0):
            left = (ds_v, p_v)[which]
            right = (q_v, o_v)[which]
            total = jnp.dot(left[...], right[j], preferred_element_type=F32)
            if which == 0:
                total = total * scale
            keep[j, which] = total.reshape(outer, 2, piece, HEAD_DIM)
            part[j, which] = keep[j, which, :, 1 - me_lo].astype(BF16)
            x_copy(j, which).start()
            if which == 1:
                @pl.when(j > 0)
                def _():
                    pair_sum(j - 1)

    def outer_sum(j):
        for which in (1, 0):
            for step in range(1, outer):
                z_copy(j, step, which).wait()
            total = keep[j, which, me_hi, me_lo]
            for step in range(1, outer):
                total = total + z_in[j, step - 1, which].astype(F32)
            for h in range(head_group):
                h_out[j, which, h] = total[h * share : (h + 1) * share].astype(BF16)
            for step in head_steps:
                h_copy(j, step, which).start()
            cols = pl.ds(pl.multiple_of((me_h * heads + j) * HEAD_DIM, HEAD_DIM), HEAD_DIM)
            (gk_ref, gv_ref)[which][:, cols] = h_out[j, which, me_h]

    def turn(t, carry):
        @pl.when(t < heads)
        def _():
            work(t)

        @pl.when(t == heads)
        def _():
            pair_sum(t - 1)

        @pl.when(t >= 2)
        def _():
            outer_sum(t - 2)

        return carry

    lax.fori_loop(0, heads + 2, turn, 0)

    def finish(j, carry):
        forwards_sent(j)
        for which in range(2):
            out_copy(j, which).wait()
            for step in head_steps:
                h_copy(j, step, which).wait()
        return carry

    lax.fori_loop(0, heads, finish, 0)


def per_device(queries, mem_keys, mem_values, grad_out):
    head_group = lax.axis_size("head")
    query_group = lax.axis_size("query")
    mem_rows, full_width = mem_keys.shape
    rows, local_width = queries.shape
    heads = local_width // HEAD_DIM
    memory = mem_rows * head_group
    outer = query_group // 2
    share = memory // (query_group * head_group)
    piece = head_group * share
    block = math.gcd(rows, 256)
    sizes = (heads, head_group, outer, rows, mem_rows, share, block)
    big = jax.ShapeDtypeStruct((rows, local_width), BF16)
    small = jax.ShapeDtypeStruct((share, full_width), BF16)
    flops = 12 * rows * memory * local_width
    anywhere = pl.BlockSpec(memory_space=pl.ANY)
    vmem = pl.BlockSpec(memory_space=pltpu.VMEM)
    dma = pltpu.SemaphoreType.DMA
    attended, dq, grad_keys, grad_values = pl.pallas_call(
        functools.partial(kernel, sizes),
        out_shape=(big, big, small, small),
        in_specs=[pl.BlockSpec(memory_space=pltpu.HBM)] * 4,
        out_specs=(anywhere, anywhere, vmem, vmem),
        scratch_shapes=[
            pltpu.VMEM((heads, rows, HEAD_DIM), BF16),
            pltpu.VMEM((heads, rows, HEAD_DIM), BF16),
            pltpu.VMEM((heads, memory, HEAD_DIM), BF16),
            pltpu.VMEM((heads, memory, HEAD_DIM), BF16),
            pltpu.VMEM((HEAD_DIM, memory), BF16),
            pltpu.VMEM((HEAD_DIM, memory), BF16),
            pltpu.VMEM((memory, rows), BF16),
            pltpu.VMEM((memory, rows), BF16),
            pltpu.VMEM((heads, rows, HEAD_DIM), BF16),
            pltpu.VMEM((heads, rows, HEAD_DIM), BF16),
            pltpu.VMEM((heads, 2, outer, piece, HEAD_DIM), BF16),
            pltpu.VMEM((heads, 2, outer, 2, piece, HEAD_DIM), F32),
            pltpu.VMEM((heads, 2, outer, piece, HEAD_DIM), BF16),
            pltpu.VMEM((heads, outer - 1, 2, piece, HEAD_DIM), BF16),
            pltpu.VMEM((heads, outer - 1, 2, piece, HEAD_DIM), BF16),
            pltpu.VMEM((heads, 2, head_group, share, HEAD_DIM), BF16),
            dma((heads, head_group - 1, 2)),
            dma((heads, head_group - 1, 2)),
            dma((heads, head_group - 1, 2)),
            dma((heads, 2)),
            dma((heads, 2)),
            dma((heads, 2)),
            dma((heads, 2)),
            dma((heads, 2)),
            dma((heads, outer - 1, 2)),
            dma((heads, outer - 1, 2)),
            dma((heads, head_group - 1, 2)),
            dma((heads, head_group - 1, 2)),
        ],
        compiler_params=pltpu.CompilerParams(
            collective_id=0, has_side_effects=True, vmem_limit_bytes=56 * 1024 * 1024
        ),
        cost_estimate=pl.CostEstimate(
            flops=flops,
            bytes_accessed=8 * rows * local_width + 4 * mem_rows * full_width,
            transcendentals=rows * memory * heads,
        ),
    )(queries, mem_keys, mem_values, grad_out)
    return attended, dq * jnp.bfloat16(HEAD_DIM ** -0.5), grad_keys, grad_values


def solution(mesh):
    in_specs = (P("query", "head"), P("head", None), P("head", None), P("query", "head"))
    out_specs = (
        P("query", "head"),
        P("query", "head"),
        P(("query", "head"), None),
        P(("query", "head"), None),
    )
    return jax.shard_map(
        per_device, mesh=mesh, in_specs=in_specs, out_specs=out_specs, check_vma=False
    )
```

```python
import functools
import math

import jax
import jax.numpy as jnp
from jax import lax
from jax.experimental import pallas as pl
from jax.experimental.pallas import tpu as pltpu
from jax.sharding import PartitionSpec as P

HEAD_DIM = 256
MESH = pl.DeviceIdType.MESH
F32 = jnp.float32
BF16 = jnp.bfloat16
NT = (((1,), (1,)), ((), ()))


def kernel(
    sizes,
    q_hbm, k_hbm, v_hbm, o_hbm,
    att_hbm, dq_hbm, gk_ref, gv_ref,
    q_v, o_v, k_v, v_v, kt_v, vt_v, p_v, ds_v, att_v, dq_v,
    part, keep, x_in, z_out, z_in, h_out,
    kv_send, kv_recv, kv_own, qo_sem, out_sem,
    x_send, x_recv, z_send, z_recv, h_send, h_recv,
):
    heads, head_group, outer, rows, mem_rows, share, block = sizes
    memory = mem_rows * head_group
    piece = head_group * share
    me_q, me_h = lax.axis_index("query"), lax.axis_index("head")
    me_hi, me_lo = me_q // 2, me_q % 2
    scale = HEAD_DIM ** -0.5

    def head_peer(step):
        return me_q, lax.rem(me_h + step, head_group)

    def pair_peer():
        return me_hi * 2 + 1 - me_lo, me_h

    def outer_peer(step):
        return lax.rem(me_hi + step, outer) * 2 + me_lo, me_h

    head_steps = [s for s in range(2, head_group)] + [1]

    def kv_copy(j, step, which):
        src, dst = ((k_hbm, k_v), (v_hbm, v_v))[which]
        peer = head_peer(step)
        cols = pl.ds(pl.multiple_of((peer[1] * heads + j) * HEAD_DIM, HEAD_DIM), HEAD_DIM)
        mine = pl.ds(pl.multiple_of(me_h * mem_rows, mem_rows), mem_rows)
        return pltpu.make_async_remote_copy(
            src_ref=src.at[:, cols],
            dst_ref=dst.at[j, mine, :],
            send_sem=kv_send.at[j, step - 1, which],
            recv_sem=kv_recv.at[j, step - 1, which],
            device_id=peer,
            device_id_type=MESH,
        )

    def kv_local(j, which):
        src, dst = ((k_hbm, k_v), (v_hbm, v_v))[which]
        cols = pl.ds(pl.multiple_of((me_h * heads + j) * HEAD_DIM, HEAD_DIM), HEAD_DIM)
        mine = pl.ds(pl.multiple_of(me_h * mem_rows, mem_rows), mem_rows)
        return pltpu.make_async_copy(src.at[:, cols], dst.at[j, mine, :], kv_own.at[j, which])

    def qo_copy(j, which):
        src, dst = ((q_hbm, q_v), (o_hbm, o_v))[which]
        cols = pl.ds(pl.multiple_of(j * HEAD_DIM, HEAD_DIM), HEAD_DIM)
        return pltpu.make_async_copy(src.at[:, cols], dst.at[j], qo_sem.at[j, which])

    def out_copy(j, which):
        src, dst = ((att_v, att_hbm), (dq_v, dq_hbm))[which]
        cols = pl.ds(pl.multiple_of(j * HEAD_DIM, HEAD_DIM), HEAD_DIM)
        return pltpu.make_async_copy(src.at[j], dst.at[:, cols], out_sem.at[j, which])

    def x_copy(j, which):
        return pltpu.make_async_remote_copy(
            src_ref=part.at[j, which],
            dst_ref=x_in.at[j, which],
            send_sem=x_send.at[j, which],
            recv_sem=x_recv.at[j, which],
            device_id=pair_peer(),
            device_id_type=MESH,
        )

    def z_copy(j, step, which):
        return pltpu.make_async_remote_copy(
            src_ref=z_out.at[j, step - 1, which],
            dst_ref=z_in.at[j, step - 1, which],
            send_sem=z_send.at[j, step - 1, which],
            recv_sem=z_recv.at[j, step - 1, which],
            device_id=outer_peer(step),
            device_id_type=MESH,
        )

    def h_copy(j, step, which):
        peer = head_peer(step)
        cols = pl.ds(pl.multiple_of((me_h * heads + j) * HEAD_DIM, HEAD_DIM), HEAD_DIM)
        return pltpu.make_async_remote_copy(
            src_ref=h_out.at[j, which, peer[1]],
            dst_ref=(gk_ref, gv_ref)[which].at[:, cols],
            send_sem=h_send.at[j, step - 1, which],
            recv_sem=h_recv.at[j, step - 1, which],
            device_id=peer,
            device_id_type=MESH,
        )

    def over_memory(reduce, array):
        groups = array.reshape(memory // 64, 64, block)
        return reduce(reduce(groups, axis=0), axis=0, keepdims=True)

    barrier = pltpu.get_barrier_semaphore()
    peers = [head_peer(s) for s in range(1, head_group)]
    peers += [pair_peer()] + [outer_peer(s) for s in range(1, outer)]
    for peer in peers:
        pl.semaphore_signal(barrier, inc=1, device_id=peer, device_id_type=MESH)
    for which in range(2):
        kv_local(0, which).start()
        qo_copy(0, which).start()
    pl.semaphore_wait(barrier, len(peers))

    def send_inputs(j):
        for step in head_steps:
            for which in range(2):
                kv_copy(j, step, which).start()

    def inputs_sent(j):
        for step in head_steps:
            for which in range(2):
                kv_copy(j, step, which).wait_send()

    send_inputs(0)

    def start_local(j, carry):
        for which in range(2):
            kv_local(j, which).start()
            qo_copy(j, which).start()
        return carry

    lax.fori_loop(1, heads, start_local, 0)
    inputs_sent(0)
    if heads > 1:
        send_inputs(1)

    def work(j):
        for which in range(2):
            kv_local(j, which).wait()
            qo_copy(j, which).wait()
            for step in head_steps:
                kv_copy(j, step, which).wait_recv()
        kt_v[...] = k_v[j].T
        vt_v[...] = v_v[j].T

        def products(r):
            at = slice(r * block, (r + 1) * block)
            scores = lax.dot_general(k_v[j], q_v[j, at, :], NT, preferred_element_type=F32)
            dprobs = lax.dot_general(v_v[j], o_v[j, at, :], NT, preferred_element_type=F32)
            return scores, dprobs

        blocks = rows // block
        ahead = products(0)
        for r in range(blocks):
            scores, dprobs = ahead
            if r + 1 < blocks:
                ahead = products(r + 1)
            at = slice(r * block, (r + 1) * block)
            top = over_memory(jnp.max, scores)
            weights = jnp.exp2((scores - top) * (scale * math.log2(math.e)))
            probs = (weights * (1.0 / over_memory(jnp.sum, weights))).astype(BF16)
            p_v[:, at] = probs
            delta = over_memory(jnp.sum, probs.astype(F32) * dprobs)
            dscores = probs * (dprobs - delta).astype(BF16)
            ds_v[:, at] = dscores
            att = jnp.dot(vt_v[...], probs, preferred_element_type=F32).astype(BF16)
            att_v[j, at, :] = att.T
            dq = (jnp.dot(kt_v[...], dscores, preferred_element_type=F32) * scale).astype(BF16)
            dq_v[j, at, :] = dq.T

        for which in range(2):
            out_copy(j, which).start()

        for which in (1, 0):
            left = (ds_v, p_v)[which]
            right = (q_v, o_v)[which]
            total = jnp.dot(left[...], right[j], preferred_element_type=F32)
            if which == 0:
                total = total * scale
            keep[j, which] = total.reshape(outer, 2, piece, HEAD_DIM)
            part[j, which] = keep[j, which, :, 1 - me_lo].astype(BF16)
            x_copy(j, which).start()

        @pl.when(j + 1 < heads)
        def _():
            inputs_sent(j + 1)

        @pl.when(j + 2 < heads)
        def _():
            send_inputs(j + 2)

    def pair_sum(j):
        for which in (1, 0):
            x_copy(j, which).wait()
            for step in range(1, outer):
                hi = lax.rem(me_hi + step, outer)
                total = keep[j, which, hi, me_lo] + x_in[j, which, hi].astype(F32)
                z_out[j, step - 1, which] = total.astype(BF16)
                z_copy(j, step, which).start()
            keep[j, which, me_hi, me_lo] += x_in[j, which, me_hi].astype(F32)

    def outer_sum(j):
        for which in (1, 0):
            for step in range(1, outer):
                z_copy(j, step, which).wait()
            total = keep[j, which, me_hi, me_lo]
            for step in range(1, outer):
                total = total + z_in[j, step - 1, which].astype(F32)
            for h in range(head_group):
                h_out[j, which, h] = total[h * share : (h + 1) * share].astype(BF16)
            for step in head_steps:
                h_copy(j, step, which).start()
            cols = pl.ds(pl.multiple_of((me_h * heads + j) * HEAD_DIM, HEAD_DIM), HEAD_DIM)
            (gk_ref, gv_ref)[which][:, cols] = h_out[j, which, me_h]

    def turn(t, carry):
        @pl.when(t < heads)
        def _():
            work(t)

        @pl.when(jnp.logical_and(t >= 1, t <= heads))
        def _():
            pair_sum(t - 1)

        @pl.when(t >= 2)
        def _():
            outer_sum(t - 2)

        return carry

    lax.fori_loop(0, heads + 2, turn, 0)

    def finish(j, carry):
        for which in range(2):
            out_copy(j, which).wait()
            for step in head_steps:
                h_copy(j, step, which).wait()
        return carry

    lax.fori_loop(0, heads, finish, 0)


def per_device(queries, mem_keys, mem_values, grad_out):
    head_group = lax.axis_size("head")
    query_group = lax.axis_size("query")
    mem_rows, full_width = mem_keys.shape
    rows, local_width = queries.shape
    heads = local_width // HEAD_DIM
    memory = mem_rows * head_group
    outer = query_group // 2
    share = memory // (query_group * head_group)
    piece = head_group * share
    block = math.gcd(rows, 256)
    sizes = (heads, head_group, outer, rows, mem_rows, share, block)
    big = jax.ShapeDtypeStruct((rows, local_width), BF16)
    small = jax.ShapeDtypeStruct((share, full_width), BF16)
    flops = 12 * rows * memory * local_width
    anywhere = pl.BlockSpec(memory_space=pl.ANY)
    vmem = pl.BlockSpec(memory_space=pltpu.VMEM)
    dma = pltpu.SemaphoreType.DMA
    return tuple(pl.pallas_call(
        functools.partial(kernel, sizes),
        out_shape=(big, big, small, small),
        in_specs=[pl.BlockSpec(memory_space=pltpu.HBM)] * 4,
        out_specs=(anywhere, anywhere, vmem, vmem),
        scratch_shapes=[
            pltpu.VMEM((heads, rows, HEAD_DIM), BF16),
            pltpu.VMEM((heads, rows, HEAD_DIM), BF16),
            pltpu.VMEM((heads, memory, HEAD_DIM), BF16),
            pltpu.VMEM((heads, memory, HEAD_DIM), BF16),
            pltpu.VMEM((HEAD_DIM, memory), BF16),
            pltpu.VMEM((HEAD_DIM, memory), BF16),
            pltpu.VMEM((memory, rows), BF16),
            pltpu.VMEM((memory, rows), BF16),
            pltpu.VMEM((heads, rows, HEAD_DIM), BF16),
            pltpu.VMEM((heads, rows, HEAD_DIM), BF16),
            pltpu.VMEM((heads, 2, outer, piece, HEAD_DIM), BF16),
            pltpu.VMEM((heads, 2, outer, 2, piece, HEAD_DIM), F32),
            pltpu.VMEM((heads, 2, outer, piece, HEAD_DIM), BF16),
            pltpu.VMEM((heads, outer - 1, 2, piece, HEAD_DIM), BF16),
            pltpu.VMEM((heads, outer - 1, 2, piece, HEAD_DIM), BF16),
            pltpu.VMEM((heads, 2, head_group, share, HEAD_DIM), BF16),
            dma((heads, head_group - 1, 2)),
            dma((heads, head_group - 1, 2)),
            dma((heads, 2)),
            dma((heads, 2)),
            dma((heads, 2)),
            dma((heads, 2)),
            dma((heads, 2)),
            dma((heads, outer - 1, 2)),
            dma((heads, outer - 1, 2)),
            dma((heads, head_group - 1, 2)),
            dma((heads, head_group - 1, 2)),
        ],
        compiler_params=pltpu.CompilerParams(
            collective_id=0, has_side_effects=True, vmem_limit_bytes=56 * 1024 * 1024
        ),
        cost_estimate=pl.CostEstimate(
            flops=flops,
            bytes_accessed=8 * rows * local_width + 4 * mem_rows * full_width,
            transcendentals=rows * memory * heads,
        ),
    )(queries, mem_keys, mem_values, grad_out))


def solution(mesh):
    in_specs = (P("query", "head"), P("head", None), P("head", None), P("query", "head"))
    out_specs = (
        P("query", "head"),
        P("query", "head"),
        P(("query", "head"), None),
        P(("query", "head"), None),
    )
    return jax.shard_map(
        per_device, mesh=mesh, in_specs=in_specs, out_specs=out_specs, check_vma=False
    )
```

```python
import functools
import math

import jax
import jax.numpy as jnp
from jax import lax
from jax.experimental import pallas as pl
from jax.experimental.pallas import tpu as pltpu
from jax.sharding import PartitionSpec as P

HEAD_DIM = 256
MESH = pl.DeviceIdType.MESH
F32 = jnp.float32
BF16 = jnp.bfloat16
NT = (((1,), (1,)), ((), ()))


def kernel(
    sizes,
    q_hbm, k_hbm, v_hbm, o_hbm,
    att_hbm, dq_hbm, gk_ref, gv_ref,
    q_v, o_v, k_v, v_v, kt_v, vt_v, p_v, ds_v, att_v, dq_v,
    part, keep, x_in, near_out, near_in, z_out, z_in, h_out,
    kv_send, kv_recv, kv_own, qo_sem, out_sem,
    x_send, x_recv, near_send, near_recv, z_send, z_recv, h_send, h_recv,
):
    heads, head_group, outer, rows, mem_rows, share, block = sizes
    memory = mem_rows * head_group
    piece = head_group * share
    me_q, me_h = lax.axis_index("query"), lax.axis_index("head")
    me_hi, me_lo = me_q // 2, me_q % 2
    me_far, me_near = me_hi // 2, me_hi % 2
    far = outer // 2
    scale = HEAD_DIM ** -0.5

    def head_peer(step):
        return me_q, lax.rem(me_h + step, head_group)

    def pair_peer():
        return me_hi * 2 + 1 - me_lo, me_h

    def near_peer():
        return (me_far * 2 + 1 - me_near) * 2 + me_lo, me_h

    def far_peer(step):
        return (lax.rem(me_far + step, far) * 2 + me_near) * 2 + me_lo, me_h

    head_steps = [s for s in range(2, head_group)] + [1]

    def kv_copy(j, step, which):
        src, dst = ((k_hbm, k_v), (v_hbm, v_v))[which]
        peer = head_peer(step)
        cols = pl.ds(pl.multiple_of((peer[1] * heads + j) * HEAD_DIM, HEAD_DIM), HEAD_DIM)
        mine = pl.ds(pl.multiple_of(me_h * mem_rows, mem_rows), mem_rows)
        return pltpu.make_async_remote_copy(
            src_ref=src.at[:, cols],
            dst_ref=dst.at[j, mine, :],
            send_sem=kv_send.at[j, step - 1, which],
            recv_sem=kv_recv.at[j, step - 1, which],
            device_id=peer,
            device_id_type=MESH,
        )

    def kv_local(j, which):
        src, dst = ((k_hbm, k_v), (v_hbm, v_v))[which]
        cols = pl.ds(pl.multiple_of((me_h * heads + j) * HEAD_DIM, HEAD_DIM), HEAD_DIM)
        mine = pl.ds(pl.multiple_of(me_h * mem_rows, mem_rows), mem_rows)
        return pltpu.make_async_copy(src.at[:, cols], dst.at[j, mine, :], kv_own.at[j, which])

    def qo_copy(j, which):
        src, dst = ((q_hbm, q_v), (o_hbm, o_v))[which]
        cols = pl.ds(pl.multiple_of(j * HEAD_DIM, HEAD_DIM), HEAD_DIM)
        return pltpu.make_async_copy(src.at[:, cols], dst.at[j], qo_sem.at[j, which])

    def out_copy(j, which):
        src, dst = ((att_v, att_hbm), (dq_v, dq_hbm))[which]
        cols = pl.ds(pl.multiple_of(j * HEAD_DIM, HEAD_DIM), HEAD_DIM)
        return pltpu.make_async_copy(src.at[j], dst.at[:, cols], out_sem.at[j, which])

    def x_copy(j, which):
        return pltpu.make_async_remote_copy(
            src_ref=part.at[j, which],
            dst_ref=x_in.at[j, which],
            send_sem=x_send.at[j, which],
            recv_sem=x_recv.at[j, which],
            device_id=pair_peer(),
            device_id_type=MESH,
        )

    def near_copy(j, which):
        return pltpu.make_async_remote_copy(
            src_ref=near_out.at[j, which],
            dst_ref=near_in.at[j, which],
            send_sem=near_send.at[j, which],
            recv_sem=near_recv.at[j, which],
            device_id=near_peer(),
            device_id_type=MESH,
        )

    def z_copy(j, step, which):
        return pltpu.make_async_remote_copy(
            src_ref=z_out.at[j, step - 1, which],
            dst_ref=z_in.at[j, step - 1, which],
            send_sem=z_send.at[j, step - 1, which],
            recv_sem=z_recv.at[j, step - 1, which],
            device_id=far_peer(step),
            device_id_type=MESH,
        )

    def h_copy(j, step, which):
        peer = head_peer(step)
        cols = pl.ds(pl.multiple_of((me_h * heads + j) * HEAD_DIM, HEAD_DIM), HEAD_DIM)
        return pltpu.make_async_remote_copy(
            src_ref=h_out.at[j, which, peer[1]],
            dst_ref=(gk_ref, gv_ref)[which].at[:, cols],
            send_sem=h_send.at[j, step - 1, which],
            recv_sem=h_recv.at[j, step - 1, which],
            device_id=peer,
            device_id_type=MESH,
        )

    def over_memory(reduce, array):
        groups = array.reshape(memory // 64, 64, block)
        return reduce(reduce(groups, axis=0), axis=0, keepdims=True)

    barrier = pltpu.get_barrier_semaphore()
    peers = [head_peer(s) for s in range(1, head_group)]
    peers += [pair_peer(), near_peer()] + [far_peer(s) for s in range(1, far)]
    for peer in peers:
        pl.semaphore_signal(barrier, inc=1, device_id=peer, device_id_type=MESH)
    for which in range(2):
        kv_local(0, which).start()
        qo_copy(0, which).start()
    pl.semaphore_wait(barrier, len(peers))

    def send_inputs(j):
        for step in head_steps:
            for which in range(2):
                kv_copy(j, step, which).start()

    def inputs_sent(j):
        for step in head_steps:
            for which in range(2):
                kv_copy(j, step, which).wait_send()

    send_inputs(0)

    def start_local(j, carry):
        for which in range(2):
            kv_local(j, which).start()
            qo_copy(j, which).start()
        return carry

    lax.fori_loop(1, heads, start_local, 0)
    inputs_sent(0)
    if heads > 1:
        send_inputs(1)

    def work(j):
        for which in range(2):
            kv_local(j, which).wait()
            qo_copy(j, which).wait()
            for step in head_steps:
                kv_copy(j, step, which).wait_recv()
        kt_v[...] = k_v[j].T
        vt_v[...] = v_v[j].T

        def products(r):
            at = slice(r * block, (r + 1) * block)
            scores = lax.dot_general(k_v[j], q_v[j, at, :], NT, preferred_element_type=F32)
            dprobs = lax.dot_general(v_v[j], o_v[j, at, :], NT, preferred_element_type=F32)
            return scores, dprobs

        blocks = rows // block
        ahead = products(0)
        for r in range(blocks):
            scores, dprobs = ahead
            if r + 1 < blocks:
                ahead = products(r + 1)
            at = slice(r * block, (r + 1) * block)
            top = over_memory(jnp.max, scores)
            weights = jnp.exp2((scores - top) * (scale * math.log2(math.e)))
            probs = (weights * (1.0 / over_memory(jnp.sum, weights))).astype(BF16)
            p_v[:, at] = probs
            delta = over_memory(jnp.sum, probs.astype(F32) * dprobs)
            dscores = probs * (dprobs - delta).astype(BF16)
            ds_v[:, at] = dscores
            att = jnp.dot(vt_v[...], probs, preferred_element_type=F32).astype(BF16)
            att_v[j, at, :] = att.T
            dq = (jnp.dot(kt_v[...], dscores, preferred_element_type=F32) * scale).astype(BF16)
            dq_v[j, at, :] = dq.T

        for which in range(2):
            out_copy(j, which).start()

        for which in (1, 0):
            left = (ds_v, p_v)[which]
            right = (q_v, o_v)[which]
            total = jnp.dot(left[...], right[j], preferred_element_type=F32)
            if which == 0:
                total = total * scale
            keep[j, which] = total.reshape(outer, 2, piece, HEAD_DIM)
            part[j, which] = keep[j, which, :, 1 - me_lo].astype(BF16)
            x_copy(j, which).start()

        @pl.when(j + 1 < heads)
        def _():
            inputs_sent(j + 1)

        @pl.when(j + 2 < heads)
        def _():
            send_inputs(j + 2)

    def pair_sum(j):
        for which in (1, 0):
            x_copy(j, which).wait()
            for f in range(far):
                hi = f * 2 + 1 - me_near
                total = keep[j, which, hi, me_lo] + x_in[j, which, hi].astype(F32)
                near_out[j, which, f] = total.astype(BF16)
            near_copy(j, which).start()
            for f in range(far):
                hi = f * 2 + me_near
                keep[j, which, hi, me_lo] += x_in[j, which, hi].astype(F32)

    def near_sum(j):
        for which in (1, 0):
            near_copy(j, which).wait()
            for step in range(1, far):
                f = lax.rem(me_far + step, far)
                total = keep[j, which, f * 2 + me_near, me_lo]
                z_out[j, step - 1, which] = (total + near_in[j, which, f].astype(F32)).astype(BF16)
                z_copy(j, step, which).start()
            keep[j, which, me_hi, me_lo] += near_in[j, which, me_far].astype(F32)

    def outer_sum(j):
        for which in (1, 0):
            for step in range(1, far):
                z_copy(j, step, which).wait()
            total = keep[j, which, me_hi, me_lo]
            for step in range(1, far):
                total = total + z_in[j, step - 1, which].astype(F32)
            for h in range(head_group):
                h_out[j, which, h] = total[h * share : (h + 1) * share].astype(BF16)
            for step in head_steps:
                h_copy(j, step, which).start()
            cols = pl.ds(pl.multiple_of((me_h * heads + j) * HEAD_DIM, HEAD_DIM), HEAD_DIM)
            (gk_ref, gv_ref)[which][:, cols] = h_out[j, which, me_h]

    def turn(t, carry):
        @pl.when(t < heads)
        def _():
            work(t)

        for lag, stage in ((1, pair_sum), (2, near_sum), (3, outer_sum)):
            @pl.when(jnp.logical_and(t >= lag, t < heads + lag))
            def _():
                stage(t - lag)

        return carry

    lax.fori_loop(0, heads + 3, turn, 0)

    def finish(j, carry):
        for which in range(2):
            out_copy(j, which).wait()
            for step in head_steps:
                h_copy(j, step, which).wait()
        return carry

    lax.fori_loop(0, heads, finish, 0)


def per_device(queries, mem_keys, mem_values, grad_out):
    head_group = lax.axis_size("head")
    query_group = lax.axis_size("query")
    mem_rows, full_width = mem_keys.shape
    rows, local_width = queries.shape
    heads = local_width // HEAD_DIM
    memory = mem_rows * head_group
    outer = query_group // 2
    share = memory // (query_group * head_group)
    piece = head_group * share
    block = math.gcd(rows, 256)
    sizes = (heads, head_group, outer, rows, mem_rows, share, block)
    big = jax.ShapeDtypeStruct((rows, local_width), BF16)
    small = jax.ShapeDtypeStruct((share, full_width), BF16)
    flops = 12 * rows * memory * local_width
    anywhere = pl.BlockSpec(memory_space=pl.ANY)
    vmem = pl.BlockSpec(memory_space=pltpu.VMEM)
    dma = pltpu.SemaphoreType.DMA
    return tuple(pl.pallas_call(
        functools.partial(kernel, sizes),
        out_shape=(big, big, small, small),
        in_specs=[pl.BlockSpec(memory_space=pltpu.HBM)] * 4,
        out_specs=(anywhere, anywhere, vmem, vmem),
        scratch_shapes=[
            pltpu.VMEM((heads, rows, HEAD_DIM), BF16),
            pltpu.VMEM((heads, rows, HEAD_DIM), BF16),
            pltpu.VMEM((heads, memory, HEAD_DIM), BF16),
            pltpu.VMEM((heads, memory, HEAD_DIM), BF16),
            pltpu.VMEM((HEAD_DIM, memory), BF16),
            pltpu.VMEM((HEAD_DIM, memory), BF16),
            pltpu.VMEM((memory, rows), BF16),
            pltpu.VMEM((memory, rows), BF16),
            pltpu.VMEM((heads, rows, HEAD_DIM), BF16),
            pltpu.VMEM((heads, rows, HEAD_DIM), BF16),
            pltpu.VMEM((heads, 2, outer, piece, HEAD_DIM), BF16),
            pltpu.VMEM((heads, 2, outer, 2, piece, HEAD_DIM), F32),
            pltpu.VMEM((heads, 2, outer, piece, HEAD_DIM), BF16),
            pltpu.VMEM((heads, 2, outer // 2, piece, HEAD_DIM), BF16),
            pltpu.VMEM((heads, 2, outer // 2, piece, HEAD_DIM), BF16),
            pltpu.VMEM((heads, outer // 2 - 1, 2, piece, HEAD_DIM), BF16),
            pltpu.VMEM((heads, outer // 2 - 1, 2, piece, HEAD_DIM), BF16),
            pltpu.VMEM((heads, 2, head_group, share, HEAD_DIM), BF16),
            dma((heads, head_group - 1, 2)),
            dma((heads, head_group - 1, 2)),
            dma((heads, 2)),
            dma((heads, 2)),
            dma((heads, 2)),
            dma((heads, 2)),
            dma((heads, 2)),
            dma((heads, 2)),
            dma((heads, 2)),
            dma((heads, outer // 2 - 1, 2)),
            dma((heads, outer // 2 - 1, 2)),
            dma((heads, head_group - 1, 2)),
            dma((heads, head_group - 1, 2)),
        ],
        compiler_params=pltpu.CompilerParams(
            collective_id=0, has_side_effects=True, vmem_limit_bytes=56 * 1024 * 1024
        ),
        cost_estimate=pl.CostEstimate(
            flops=flops,
            bytes_accessed=8 * rows * local_width + 4 * mem_rows * full_width,
            transcendentals=rows * memory * heads,
        ),
    )(queries, mem_keys, mem_values, grad_out))


def solution(mesh):
    in_specs = (P("query", "head"), P("head", None), P("head", None), P("query", "head"))
    out_specs = (
        P("query", "head"),
        P("query", "head"),
        P(("query", "head"), None),
        P(("query", "head"), None),
    )
    return jax.shard_map(
        per_device, mesh=mesh, in_specs=in_specs, out_specs=out_specs, check_vma=False
    )
```

```python
import functools
import math

import jax
import jax.numpy as jnp
from jax import lax
from jax.experimental import pallas as pl
from jax.experimental.pallas import tpu as pltpu
from jax.sharding import PartitionSpec as P

HEAD_DIM = 256
MESH = pl.DeviceIdType.MESH
F32 = jnp.float32
BF16 = jnp.bfloat16
NT = (((1,), (1,)), ((), ()))


def kernel(
    sizes,
    q_hbm, k_hbm, v_hbm, o_hbm,
    att_hbm, dq_hbm, gk_ref, gv_ref,
    q_v, o_v, k_v, v_v, kt_v, vt_v, p_v, ds_v, att_v, dq_v,
    part, keep, x_in, z_out, z_in, h_out, eye_v,
    kv_send, kv_recv, kv_own, qo_sem, out_sem,
    x_send, x_recv, z_send, z_recv, h_send, h_recv,
):
    heads, head_group, outer, rows, mem_rows, share, block = sizes
    memory = mem_rows * head_group
    piece = head_group * share
    me_q, me_h = lax.axis_index("query"), lax.axis_index("head")
    me_hi, me_lo = me_q // 2, me_q % 2
    scale = HEAD_DIM ** -0.5

    def head_peer(step):
        return me_q, lax.rem(me_h + step, head_group)

    def pair_peer():
        return me_hi * 2 + 1 - me_lo, me_h

    def outer_peer(step):
        return lax.rem(me_hi + step, outer) * 2 + me_lo, me_h

    head_steps = [s for s in range(2, head_group)] + [1]

    def kv_copy(j, step, which):
        src, dst = ((k_hbm, k_v), (v_hbm, v_v))[which]
        peer = head_peer(step)
        cols = pl.ds(pl.multiple_of((peer[1] * heads + j) * HEAD_DIM, HEAD_DIM), HEAD_DIM)
        mine = pl.ds(pl.multiple_of(me_h * mem_rows, mem_rows), mem_rows)
        return pltpu.make_async_remote_copy(
            src_ref=src.at[:, cols],
            dst_ref=dst.at[j, mine, :],
            send_sem=kv_send.at[j, step - 1, which],
            recv_sem=kv_recv.at[j, step - 1, which],
            device_id=peer,
            device_id_type=MESH,
        )

    def kv_local(j, which):
        src, dst = ((k_hbm, k_v), (v_hbm, v_v))[which]
        cols = pl.ds(pl.multiple_of((me_h * heads + j) * HEAD_DIM, HEAD_DIM), HEAD_DIM)
        mine = pl.ds(pl.multiple_of(me_h * mem_rows, mem_rows), mem_rows)
        return pltpu.make_async_copy(src.at[:, cols], dst.at[j, mine, :], kv_own.at[j, which])

    def qo_copy(j, which):
        src, dst = ((q_hbm, q_v), (o_hbm, o_v))[which]
        cols = pl.ds(pl.multiple_of(j * HEAD_DIM, HEAD_DIM), HEAD_DIM)
        return pltpu.make_async_copy(src.at[:, cols], dst.at[j], qo_sem.at[j, which])

    def out_copy(j, which):
        src, dst = ((att_v, att_hbm), (dq_v, dq_hbm))[which]
        cols = pl.ds(pl.multiple_of(j * HEAD_DIM, HEAD_DIM), HEAD_DIM)
        return pltpu.make_async_copy(src.at[j], dst.at[:, cols], out_sem.at[j, which])

    def x_copy(j, which):
        return pltpu.make_async_remote_copy(
            src_ref=part.at[j, which],
            dst_ref=x_in.at[j, which],
            send_sem=x_send.at[j, which],
            recv_sem=x_recv.at[j, which],
            device_id=pair_peer(),
            device_id_type=MESH,
        )

    def z_copy(j, step, which):
        return pltpu.make_async_remote_copy(
            src_ref=z_out.at[j, step - 1, which],
            dst_ref=z_in.at[j, step - 1, which],
            send_sem=z_send.at[j, step - 1, which],
            recv_sem=z_recv.at[j, step - 1, which],
            device_id=outer_peer(step),
            device_id_type=MESH,
        )

    def h_copy(j, step, which):
        peer = head_peer(step)
        cols = pl.ds(pl.multiple_of((me_h * heads + j) * HEAD_DIM, HEAD_DIM), HEAD_DIM)
        return pltpu.make_async_remote_copy(
            src_ref=h_out.at[j, which, peer[1]],
            dst_ref=(gk_ref, gv_ref)[which].at[:, cols],
            send_sem=h_send.at[j, step - 1, which],
            recv_sem=h_recv.at[j, step - 1, which],
            device_id=peer,
            device_id_type=MESH,
        )

    def over_memory(reduce, array):
        groups = array.reshape(memory // 64, 64, block)
        return reduce(reduce(groups, axis=0), axis=0, keepdims=True)

    def turned(array):
        return lax.dot_general(eye_v[...], array, NT, preferred_element_type=F32).astype(BF16)

    on = lax.broadcasted_iota(jnp.int32, (HEAD_DIM, HEAD_DIM), 0)
    across = lax.broadcasted_iota(jnp.int32, (HEAD_DIM, HEAD_DIM), 1)
    eye_v[...] = jnp.where(on == across, 1.0, 0.0).astype(BF16)

    barrier = pltpu.get_barrier_semaphore()
    peers = [head_peer(s) for s in range(1, head_group)]
    peers += [pair_peer()] + [outer_peer(s) for s in range(1, outer)]
    for peer in peers:
        pl.semaphore_signal(barrier, inc=1, device_id=peer, device_id_type=MESH)
    for which in range(2):
        kv_local(0, which).start()
        qo_copy(0, which).start()
    pl.semaphore_wait(barrier, len(peers))

    def send_inputs(j):
        for step in head_steps:
            for which in range(2):
                kv_copy(j, step, which).start()

    def inputs_sent(j):
        for step in head_steps:
            for which in range(2):
                kv_copy(j, step, which).wait_send()

    send_inputs(0)

    def start_local(j, carry):
        for which in range(2):
            kv_local(j, which).start()
            qo_copy(j, which).start()
        return carry

    lax.fori_loop(1, heads, start_local, 0)
    inputs_sent(0)
    if heads > 1:
        send_inputs(1)

    def work(j):
        for which in range(2):
            kv_local(j, which).wait()
            qo_copy(j, which).wait()
            for step in head_steps:
                kv_copy(j, step, which).wait_recv()
        kt_v[...] = turned(k_v[j])
        vt_v[...] = turned(v_v[j])

        def products(r):
            at = slice(r * block, (r + 1) * block)
            scores = lax.dot_general(k_v[j], q_v[j, at, :], NT, preferred_element_type=F32)
            dprobs = lax.dot_general(v_v[j], o_v[j, at, :], NT, preferred_element_type=F32)
            return scores, dprobs

        blocks = rows // block
        ahead = products(0)
        for r in range(blocks):
            scores, dprobs = ahead
            if r + 1 < blocks:
                ahead = products(r + 1)
            at = slice(r * block, (r + 1) * block)
            top = over_memory(jnp.max, scores)
            weights = jnp.exp2((scores - top) * (scale * math.log2(math.e)))
            probs = (weights * (1.0 / over_memory(jnp.sum, weights))).astype(BF16)
            p_v[:, at] = probs
            delta = over_memory(jnp.sum, probs.astype(F32) * dprobs)
            dscores = probs * (dprobs - delta).astype(BF16)
            ds_v[:, at] = dscores
            att = jnp.dot(vt_v[...], probs, preferred_element_type=F32).astype(BF16)
            att_v[j, at, :] = turned(att)
            dq = (jnp.dot(kt_v[...], dscores, preferred_element_type=F32) * scale).astype(BF16)
            dq_v[j, at, :] = turned(dq)

        for which in range(2):
            out_copy(j, which).start()

        for which in (1, 0):
            left = (ds_v, p_v)[which]
            right = (q_v, o_v)[which]
            total = jnp.dot(left[...], right[j], preferred_element_type=F32)
            if which == 0:
                total = total * scale
            keep[j, which] = total.reshape(outer, 2, piece, HEAD_DIM)
            part[j, which] = keep[j, which, :, 1 - me_lo].astype(BF16)
            x_copy(j, which).start()

        @pl.when(j + 1 < heads)
        def _():
            inputs_sent(j + 1)

        @pl.when(j + 2 < heads)
        def _():
            send_inputs(j + 2)

    def pair_sum(j):
        for which in (1, 0):
            x_copy(j, which).wait()
            for step in range(1, outer):
                hi = lax.rem(me_hi + step, outer)
                total = keep[j, which, hi, me_lo] + x_in[j, which, hi].astype(F32)
                z_out[j, step - 1, which] = total.astype(BF16)
                z_copy(j, step, which).start()
            keep[j, which, me_hi, me_lo] += x_in[j, which, me_hi].astype(F32)

    def outer_sum(j):
        for which in (1, 0):
            for step in range(1, outer):
                z_copy(j, step, which).wait()
            total = keep[j, which, me_hi, me_lo]
            for step in range(1, outer):
                total = total + z_in[j, step - 1, which].astype(F32)
            for h in range(head_group):
                h_out[j, which, h] = total[h * share : (h + 1) * share].astype(BF16)
            for step in head_steps:
                h_copy(j, step, which).start()
            cols = pl.ds(pl.multiple_of((me_h * heads + j) * HEAD_DIM, HEAD_DIM), HEAD_DIM)
            (gk_ref, gv_ref)[which][:, cols] = h_out[j, which, me_h]

    def turn(t, carry):
        @pl.when(t < heads)
        def _():
            work(t)

        @pl.when(jnp.logical_and(t >= 1, t <= heads))
        def _():
            pair_sum(t - 1)

        @pl.when(t >= 2)
        def _():
            outer_sum(t - 2)

        return carry

    lax.fori_loop(0, heads + 2, turn, 0)

    def finish(j, carry):
        for which in range(2):
            out_copy(j, which).wait()
            for step in head_steps:
                h_copy(j, step, which).wait()
        return carry

    lax.fori_loop(0, heads, finish, 0)


def per_device(queries, mem_keys, mem_values, grad_out):
    head_group = lax.axis_size("head")
    query_group = lax.axis_size("query")
    mem_rows, full_width = mem_keys.shape
    rows, local_width = queries.shape
    heads = local_width // HEAD_DIM
    memory = mem_rows * head_group
    outer = query_group // 2
    share = memory // (query_group * head_group)
    piece = head_group * share
    block = HEAD_DIM
    assert rows % block == 0
    sizes = (heads, head_group, outer, rows, mem_rows, share, block)
    big = jax.ShapeDtypeStruct((rows, local_width), BF16)
    small = jax.ShapeDtypeStruct((share, full_width), BF16)
    flops = 12 * rows * memory * local_width
    anywhere = pl.BlockSpec(memory_space=pl.ANY)
    vmem = pl.BlockSpec(memory_space=pltpu.VMEM)
    dma = pltpu.SemaphoreType.DMA
    return tuple(pl.pallas_call(
        functools.partial(kernel, sizes),
        out_shape=(big, big, small, small),
        in_specs=[pl.BlockSpec(memory_space=pltpu.HBM)] * 4,
        out_specs=(anywhere, anywhere, vmem, vmem),
        scratch_shapes=[
            pltpu.VMEM((heads, rows, HEAD_DIM), BF16),
            pltpu.VMEM((heads, rows, HEAD_DIM), BF16),
            pltpu.VMEM((heads, memory, HEAD_DIM), BF16),
            pltpu.VMEM((heads, memory, HEAD_DIM), BF16),
            pltpu.VMEM((HEAD_DIM, memory), BF16),
            pltpu.VMEM((HEAD_DIM, memory), BF16),
            pltpu.VMEM((memory, rows), BF16),
            pltpu.VMEM((memory, rows), BF16),
            pltpu.VMEM((heads, rows, HEAD_DIM), BF16),
            pltpu.VMEM((heads, rows, HEAD_DIM), BF16),
            pltpu.VMEM((heads, 2, outer, piece, HEAD_DIM), BF16),
            pltpu.VMEM((heads, 2, outer, 2, piece, HEAD_DIM), F32),
            pltpu.VMEM((heads, 2, outer, piece, HEAD_DIM), BF16),
            pltpu.VMEM((heads, outer - 1, 2, piece, HEAD_DIM), BF16),
            pltpu.VMEM((heads, outer - 1, 2, piece, HEAD_DIM), BF16),
            pltpu.VMEM((heads, 2, head_group, share, HEAD_DIM), BF16),
            pltpu.VMEM((HEAD_DIM, HEAD_DIM), BF16),
            dma((heads, head_group - 1, 2)),
            dma((heads, head_group - 1, 2)),
            dma((heads, 2)),
            dma((heads, 2)),
            dma((heads, 2)),
            dma((heads, 2)),
            dma((heads, 2)),
            dma((heads, outer - 1, 2)),
            dma((heads, outer - 1, 2)),
            dma((heads, head_group - 1, 2)),
            dma((heads, head_group - 1, 2)),
        ],
        compiler_params=pltpu.CompilerParams(
            collective_id=0, has_side_effects=True, vmem_limit_bytes=56 * 1024 * 1024
        ),
        cost_estimate=pl.CostEstimate(
            flops=flops,
            bytes_accessed=8 * rows * local_width + 4 * mem_rows * full_width,
            transcendentals=rows * memory * heads,
        ),
    )(queries, mem_keys, mem_values, grad_out))


def solution(mesh):
    in_specs = (P("query", "head"), P("head", None), P("head", None), P("query", "head"))
    out_specs = (
        P("query", "head"),
        P("query", "head"),
        P(("query", "head"), None),
        P(("query", "head"), None),
    )
    return jax.shard_map(
        per_device, mesh=mesh, in_specs=in_specs, out_specs=out_specs, check_vma=False
    )
```
